512 devices in a mesh: seq: 64 (over z, y), pipe: 8 (over x, core).
Axes of the slice: x: 4, y: 4, z: 16, core: 2. Of those that a mesh axis runs over, the one named last changes fastest.
Arguments:
- fresh_input: bfloat16 [384, 8192], P(None, 'seq'), may hold values from -8 to 8
- act_prev: bfloat16 [8, 384, 8192], P('pipe', None, 'seq'), may hold values from -8 to 8
- saved_input: bfloat16 [8, 384, 8192], P('pipe', None, 'seq'), may hold values from -8 to 8
- grad_next: bfloat16 [8, 128, 8192], P('pipe', None, 'seq'), may hold values from -8 to 8
- top_grad: bfloat16 [128, 8192], P(None, 'seq'), may hold values from -8 to 8
- filters: float32 [8, 128, 8192], P('pipe', None, 'seq'), may hold values from -0.0625 to 0.0625
Outputs:
- act_next: bfloat16 [8, 128, 8192], P('pipe', None, 'seq')
- grad_input: bfloat16 [8, 384, 8192], P('pipe', None, 'seq')
- filter_grad: float32 [8, 128, 8192], P('pipe', None, 'seq')
The draws below stay inside these ranges and needn't reach their ends.
All inputs are finite; a program needn't handle non-finite values.
Results may differ from the reference program's by a relative error of at most 0.015.
Values may be sent and summed in bfloat16 or wider, within the bound.
No kernel may reach another device: no remote copies, remote signals or barrier semaphores. Data moves between devices by JAX's collectives and lax.ppermute only.
A program may use at most 64 MiB of HBM per device.

```python
import jax
import jax.numpy as jnp

CH = 128
LENGTH = 8192
N_PIPE = 8


def level_of(stream_key, shape, cuts, least, largest):
    factor_of, own = 1.0, jax.random.fold_in(stream_key, 6)
    for dim, parts in cuts:
        steps = jnp.exp(jax.random.uniform(jax.random.fold_in(own, dim), (parts,), jnp.float32, least / len(cuts), largest / len(cuts)))
        factor_of = factor_of * jnp.repeat(steps, shape[dim] // parts).reshape([-1 if axis == dim else 1 for axis in range(len(shape))])
    return factor_of


def normal_values(own_key, dims, width, bound, cuts=(), dtype=jnp.bfloat16):
    values = jax.random.normal(own_key, dims, jnp.float32) * width
    if len(cuts) > 0:
        values = level_of(own_key, dims, cuts, -0.22, 0.18) * values
    return jnp.clip(values, min=-bound, max=bound).astype(dtype)


def setup_inputs(seed: int = 0) -> dict:
    arg_keys = jax.random.split(jax.random.key(seed), 7)
    fresh_input = normal_values(arg_keys[0], (3 * CH, LENGTH), 1.0, 8.0, ((1, 64),))
    act_prev = normal_values(arg_keys[1], (N_PIPE, 3 * CH, LENGTH), 1.0, 8.0, ((0, 8), (2, 64)))
    saved_input = normal_values(arg_keys[2], (N_PIPE, 3 * CH, LENGTH), 1.0, 8.0, ((0, 8), (2, 64)))
    grad_next = normal_values(arg_keys[3], (N_PIPE, CH, LENGTH), 1.0, 8.0, ((0, 8), (2, 64)))
    top_grad = normal_values(arg_keys[4], (CH, LENGTH), 1.0, 8.0, ((1, 64),))
    filters = normal_values(arg_keys[5], (N_PIPE, CH, LENGTH), LENGTH ** -0.5, 0.0625, ((0, 8), (2, 64)), jnp.float32)
    return {"fresh_input": fresh_input, "act_prev": act_prev, "saved_input": saved_input, "grad_next": grad_next, "top_grad": top_grad, "filters": filters}


def causal_conv(kernel, signal):
    length = kernel.shape[-1]
    spectrum = jnp.fft.rfft(kernel, n=2 * length) * jnp.fft.rfft(signal, n=2 * length)
    return jnp.fft.irfft(spectrum, n=2 * length)[:, :length]


def causal_corr(signal, grad_conv):
    length = signal.shape[-1]
    spectrum = jnp.conj(jnp.fft.rfft(signal, n=2 * length)) * jnp.fft.rfft(grad_conv, n=2 * length)
    return jnp.fft.irfft(spectrum, n=2 * length)[:, :length]


def section(source, stored, upstream, kernel):
    channels = kernel.shape[0]
    source_f = source.astype(jnp.float32)
    stored_f = stored.astype(jnp.float32)
    query_fwd = source_f[:channels]
    mix_fwd = source_f[channels:2 * channels] * source_f[2 * channels:]
    query_bwd = stored_f[:channels]
    key_bwd = stored_f[channels:2 * channels]
    value_bwd = stored_f[2 * channels:]
    mix_bwd = key_bwd * value_bwd
    conv_fwd = causal_conv(kernel, mix_fwd)
    conv_bwd = causal_conv(kernel, mix_bwd)
    act_next = (query_fwd * conv_fwd).astype(jnp.bfloat16)
    upstream_f = upstream.astype(jnp.float32)
    grad_query = upstream_f * conv_bwd
    grad_conv = upstream_f * query_bwd
    grad_mix = causal_corr(kernel, grad_conv)
    filter_grad = causal_corr(mix_bwd, grad_conv)
    grad_source = jnp.concatenate([grad_query, grad_mix * value_bwd, grad_mix * key_bwd]).astype(jnp.bfloat16)
    return act_next, grad_source, filter_grad


def reference(fresh_input, act_prev, saved_input, grad_next, top_grad, filters):
    results = []
    for segment_ix in range(N_PIPE):
        source = fresh_input if segment_ix == 0 else act_prev[segment_ix - 1]
        upstream = top_grad if segment_ix == N_PIPE - 1 else grad_next[segment_ix + 1]
        results.append(section(source, saved_input[segment_ix], upstream, filters[segment_ix]))
    return (jnp.stack([item[0] for item in results]), jnp.stack([item[1] for item in results]), jnp.stack([item[2] for item in results]))
```

```python
import functools

import jax
import jax.numpy as jnp
import ml_dtypes
import numpy as np
from jax import lax
from jax.experimental import pallas as pl
from jax.experimental.pallas import tpu as pltpu
from jax.sharding import PartitionSpec as P

F32 = jnp.float32
BF16 = jnp.bfloat16
PARAMS = pltpu.CompilerParams(vmem_limit_bytes=8 * 2**20)


def split_table(table):
    high = table.astype(ml_dtypes.bfloat16)
    low = (table - high.astype(np.float64)).astype(ml_dtypes.bfloat16)
    return high, low


@functools.lru_cache(maxsize=None)
def tables(blocks, width):
    length = blocks * width
    freq = np.arange(blocks)[:, None] + 0.25
    outer = 2.0 * np.pi * freq * np.arange(blocks)[None, :] / blocks
    inner = 2.0 * np.pi * (np.arange(width)[:, None] * np.arange(width)[None, :] % width) / width
    twist = 2.0 * np.pi * freq * np.arange(width)[None, :] / length
    cos_i, sin_i = np.cos(inner), np.sin(inner)
    outer_fwd = np.concatenate([np.cos(outer), -np.sin(outer)], axis=0)
    inner_fwd = np.block([[cos_i, -sin_i], [sin_i, cos_i]])
    return (
        *split_table(outer_fwd),
        *split_table(inner_fwd),
        *split_table(inner_fwd.T.copy()),
        *split_table(outer_fwd.T / length),
        np.cos(twist).astype(np.float32),
        np.sin(twist).astype(np.float32),
    )


def halves(value):
    high = value.astype(BF16)
    low = (value - high.astype(F32)).astype(BF16)
    return high, low


def dot(a, b):
    return jnp.dot(a, b, preferred_element_type=F32)


def gather_kernel(arrived, fresh, saved, returned, top, filt, out, rows):
    section = lax.axis_index("pipe")
    last = lax.axis_size("pipe") - 1
    channels = filt.shape[1]
    half = channels // 2
    for part in range(2):
        base = half * part

        def at(ref, group):
            span = pl.ds(group * channels + base, half)
            return (ref[0, span, :] if len(ref.shape) == 3 else ref[span, :]).astype(F32)

        key = jnp.where(section == 0, at(fresh, 1), at(arrived, 1))
        value = jnp.where(section == 0, at(fresh, 2), at(arrived, 2))
        upstream = jnp.where(section == last, at(top, 0), at(returned, 0))
        rows[pl.ds(0 + part, half, stride=8), :] = at(filt, 0)
        rows[pl.ds(2 + part, half, stride=8), :] = at(saved, 1) * at(saved, 2)
        rows[pl.ds(4 + part, half, stride=8), :] = key * value
        rows[pl.ds(6 + part, half, stride=8), :] = upstream * at(saved, 0)
    out[...] = rows[...].astype(BF16)


def convolve_kernel(
    blocks, x, f1h, f1l, f2h, f2l, b2h, b2l, b1h, b1l, cos_t, sin_t, out, rows
):
    rows[...] = x[...].astype(F32)
    taken = [rows[pl.ds(r, blocks, stride=8), :].astype(BF16) for r in range(8)]
    flat = jnp.concatenate(taken, axis=1)
    first = dot(f1h[...], flat) + dot(f1l[...], flat)
    width = x.shape[1]
    cosine, sine = cos_t[...], sin_t[...]
    stacked = []
    for r in range(8):
        real = first[:blocks, r * width : (r + 1) * width]
        imag = first[blocks:, r * width : (r + 1) * width]
        stacked.append(
            jnp.concatenate([real * cosine + imag * sine, imag * cosine - real * sine], axis=1)
        )
    high, low = halves(jnp.concatenate(stacked, axis=0))
    spec = dot(high, f2h[...]) + (dot(high, f2l[...]) + dot(low, f2h[...]))

    def parts_of(r):
        return (
            spec[r * blocks : (r + 1) * blocks, :width],
            spec[r * blocks : (r + 1) * blocks, width:],
        )

    products = []
    for kind in range(4):
        for part in range(2):
            filt, mix_b, mix_f, grad = (parts_of(2 * k + part) for k in range(4))
            if kind < 2:
                (ar, ai), (br, bi) = filt, (mix_f if kind == 0 else mix_b)
                pair = [ar * br - ai * bi, ar * bi + ai * br]
            else:
                (ar, ai), (br, bi) = (filt if kind == 2 else mix_b), grad
                pair = [ar * br + ai * bi, ar * bi - ai * br]
            products.append(jnp.concatenate(pair, axis=1))
    high, low = halves(jnp.concatenate(products, axis=0))
    back = dot(high, b2h[...]) + (dot(high, b2l[...]) + dot(low, b2h[...]))
    columns = []
    for r in range(8):
        real = back[r * blocks : (r + 1) * blocks, :width]
        imag = back[r * blocks : (r + 1) * blocks, width:]
        columns.append(
            jnp.concatenate([real * cosine - imag * sine, imag * cosine + real * sine], axis=0)
        )
    high, low = halves(jnp.concatenate(columns, axis=1))
    last = dot(b1h[...], high) + (dot(b1h[...], low) + dot(b1l[...], high))
    for r in range(8):
        rows[pl.ds(r, blocks, stride=8), :] = last[:, r * width : (r + 1) * width]
    out[...] = rows[...].astype(BF16)


def finish_kernel(x, arrived, fresh, saved, returned, top, act, grad_in, filt_grad, rows):
    section = lax.axis_index("pipe")
    last = lax.axis_size("pipe") - 1
    channels = act.shape[1]
    half = channels // 2
    rows[...] = x[...].astype(F32)
    for part in range(2):
        base = half * part

        def at(ref, group):
            span = pl.ds(group * channels + base, half)
            return (ref[0, span, :] if len(ref.shape) == 3 else ref[span, :]).astype(F32)

        def result(kind):
            return rows[pl.ds(2 * kind + part, half, stride=8), :]

        query = jnp.where(section == 0, at(fresh, 0), at(arrived, 0))
        upstream = jnp.where(section == last, at(top, 0), at(returned, 0))
        grad_mix = result(2)
        act[0, pl.ds(base, half), :] = (query * result(0)).astype(BF16)
        grad_in[0, pl.ds(base, half), :] = (upstream * result(1)).astype(BF16)
        grad_in[0, pl.ds(channels + base, half), :] = (grad_mix * at(saved, 2)).astype(BF16)
        grad_in[0, pl.ds(2 * channels + base, half), :] = (grad_mix * at(saved, 1)).astype(BF16)
        filt_grad[0, pl.ds(base, half), :] = result(3)


def per_device(fresh_input, act_prev, saved_input, grad_next, top_grad, filters):
    sections = lax.axis_size("pipe")
    blocks = lax.axis_size("seq")
    channels, width = filters.shape[1], filters.shape[2]
    total = 4 * channels
    arrived = lax.ppermute(act_prev, "pipe", [(i, i + 1) for i in range(sections - 1)])
    returned = lax.ppermute(grad_next, "pipe", [(i + 1, i) for i in range(sections - 1)])
    scratch = [pltpu.VMEM((total, width), F32)]
    sent = pl.pallas_call(
        gather_kernel,
        out_shape=jax.ShapeDtypeStruct((total, width), BF16),
        scratch_shapes=scratch,
        compiler_params=PARAMS,
        name="gather_rows",
    )(arrived, fresh_input, saved_input, returned, top_grad, filters)

    def trade(value):
        cut = value.reshape(blocks, total // blocks, width)
        return lax.all_to_all(cut, "seq", 0, 0).reshape(total, width)

    held = trade(sent)
    done = pl.pallas_call(
        functools.partial(convolve_kernel, blocks),
        out_shape=jax.ShapeDtypeStruct((total, width), BF16),
        scratch_shapes=scratch,
        compiler_params=PARAMS,
        name="convolve",
    )(held, *(jnp.asarray(t) for t in tables(blocks, width)))
    back = trade(done)
    return pl.pallas_call(
        finish_kernel,
        out_shape=(
            jax.ShapeDtypeStruct((1, channels, width), BF16),
            jax.ShapeDtypeStruct((1, 3 * channels, width), BF16),
            jax.ShapeDtypeStruct((1, channels, width), F32),
        ),
        scratch_shapes=scratch,
        compiler_params=PARAMS,
        name="finish",
    )(back, arrived, fresh_input, saved_input, returned, top_grad)


def solution(mesh):
    placed = (
        P(None, "seq"),
        P("pipe", None, "seq"),
        P("pipe", None, "seq"),
        P("pipe", None, "seq"),
        P(None, "seq"),
        P("pipe", None, "seq"),
    )
    return jax.shard_map(
        per_device,
        mesh=mesh,
        in_specs=placed,
        out_specs=(P("pipe", None, "seq"), P("pipe", None, "seq"), P("pipe", None, "seq")),
        check_vma=False,
    )
```

```python
import functools

import jax
import jax.numpy as jnp
import ml_dtypes
import numpy as np
from jax import lax
from jax.experimental import pallas as pl
from jax.experimental.pallas import tpu as pltpu
from jax.sharding import PartitionSpec as P

F32 = jnp.float32
BF16 = jnp.bfloat16
PARAMS = pltpu.CompilerParams(vmem_limit_bytes=8 * 2**20)


def split_table(table):
    high = table.astype(ml_dtypes.bfloat16)
    low = (table - high.astype(np.float64)).astype(ml_dtypes.bfloat16)
    return high, low


def trade_order(blocks):
    first = blocks // 2 + 2 if blocks > 4 else 0
    return [(first + i) % blocks for i in range(blocks)]


@functools.lru_cache(maxsize=None)
def tables(blocks, width):
    length = blocks * width
    freq = np.arange(blocks)[:, None] + 0.25
    outer = 2.0 * np.pi * freq * np.array(trade_order(blocks))[None, :] / blocks
    inner = 2.0 * np.pi * (np.arange(width)[:, None] * np.arange(width)[None, :] % width) / width
    twist = 2.0 * np.pi * freq * np.arange(width)[None, :] / length
    cos_i, sin_i = np.cos(inner), np.sin(inner)
    outer_fwd = np.concatenate([np.cos(outer), -np.sin(outer)], axis=0)
    inner_fwd = np.block([[cos_i, -sin_i], [sin_i, cos_i]])
    return (
        *split_table(outer_fwd),
        *split_table(inner_fwd),
        *split_table(inner_fwd.T.copy()),
        *split_table(outer_fwd.T / length),
        np.cos(twist).astype(np.float32),
        np.sin(twist).astype(np.float32),
    )


def halves(value):
    high = value.astype(BF16)
    low = (value - high.astype(F32)).astype(BF16)
    return high, low


def dot(a, b):
    return jnp.dot(a, b, preferred_element_type=F32)


def stage_kernel(fresh, saved, top, filt, fresh_v, saved_v, top_v, filt_v, sems):
    pairs = ((filt, filt_v), (saved, saved_v), (fresh, fresh_v), (top, top_v))
    copies = [pltpu.make_async_copy(a, b, sems.at[i]) for i, (a, b) in enumerate(pairs)]
    for copy in copies:
        copy.start()
    for copy in copies:
        copy.wait()


def gather_kernel(arrived, fresh, saved, returned, top, filt, out, rows):
    section = lax.axis_index("pipe")
    last = lax.axis_size("pipe") - 1
    channels = filt.shape[1]
    half = channels // 2
    for part in range(2):
        base = half * part

        def at(ref, group):
            span = pl.ds(group * channels + base, half)
            return (ref[0, span, :] if len(ref.shape) == 3 else ref[span, :]).astype(F32)

        key = jnp.where(section == 0, at(fresh, 1), at(arrived, 1))
        value = jnp.where(section == 0, at(fresh, 2), at(arrived, 2))
        upstream = jnp.where(section == last, at(top, 0), at(returned, 0))
        rows[pl.ds(0 + part, half, stride=8), :] = at(filt, 0)
        rows[pl.ds(2 + part, half, stride=8), :] = at(saved, 1) * at(saved, 2)
        rows[pl.ds(4 + part, half, stride=8), :] = key * value
        rows[pl.ds(6 + part, half, stride=8), :] = upstream * at(saved, 0)
    out[...] = rows[...].astype(BF16)


def convolve_kernel(
    blocks, x, f1h, f1l, f2h, f2l, b2h, b2l, b1h, b1l, cos_t, sin_t, out, rows
):
    rows[...] = x[...].astype(F32)
    taken = [rows[pl.ds(r, blocks, stride=8), :].astype(BF16) for r in range(8)]
    flat = jnp.concatenate(taken, axis=1)
    first = dot(f1h[...], flat) + dot(f1l[...], flat)
    width = x.shape[1]
    cosine, sine = cos_t[...], sin_t[...]
    stacked = []
    for r in range(8):
        real = first[:blocks, r * width : (r + 1) * width]
        imag = first[blocks:, r * width : (r + 1) * width]
        stacked.append(
            jnp.concatenate([real * cosine + imag * sine, imag * cosine - real * sine], axis=1)
        )
    high, low = halves(jnp.concatenate(stacked, axis=0))
    spec = dot(high, f2h[...]) + (dot(high, f2l[...]) + dot(low, f2h[...]))

    def parts_of(r):
        return (
            spec[r * blocks : (r + 1) * blocks, :width],
            spec[r * blocks : (r + 1) * blocks, width:],
        )

    products = []
    for kind in range(4):
        for part in range(2):
            filt, mix_b, mix_f, grad = (parts_of(2 * k + part) for k in range(4))
            if kind < 2:
                (ar, ai), (br, bi) = filt, (mix_f if kind == 0 else mix_b)
                pair = [ar * br - ai * bi, ar * bi + ai * br]
            else:
                (ar, ai), (br, bi) = (filt if kind == 2 else mix_b), grad
                pair = [ar * br + ai * bi, ar * bi - ai * br]
            products.append(jnp.concatenate(pair, axis=1))
    high, low = halves(jnp.concatenate(products, axis=0))
    back = dot(high, b2h[...]) + (dot(high, b2l[...]) + dot(low, b2h[...]))
    columns = []
    for r in range(8):
        real = back[r * blocks : (r + 1) * blocks, :width]
        imag = back[r * blocks : (r + 1) * blocks, width:]
        columns.append(
            jnp.concatenate([real * cosine - imag * sine, imag * cosine + real * sine], axis=0)
        )
    high, low = halves(jnp.concatenate(columns, axis=1))
    last = dot(b1h[...], high) + (dot(b1h[...], low) + dot(b1l[...], high))
    for r in range(8):
        rows[pl.ds(r, blocks, stride=8), :] = last[:, r * width : (r + 1) * width]
    out[...] = rows[...].astype(BF16)


def finish_kernel(x, arrived, fresh, saved, returned, top, act, grad_in, filt_grad, rows):
    section = lax.axis_index("pipe")
    last = lax.axis_size("pipe") - 1
    channels = act.shape[1]
    half = channels // 2
    rows[...] = x[...].astype(F32)
    for part in range(2):
        base = half * part

        def at(ref, group):
            span = pl.ds(group * channels + base, half)
            return (ref[0, span, :] if len(ref.shape) == 3 else ref[span, :]).astype(F32)

        def result(kind):
            return rows[pl.ds(2 * kind + part, half, stride=8), :]

        query = jnp.where(section == 0, at(fresh, 0), at(arrived, 0))
        upstream = jnp.where(section == last, at(top, 0), at(returned, 0))
        grad_mix = result(2)
        act[0, pl.ds(base, half), :] = (query * result(0)).astype(BF16)
        grad_in[0, pl.ds(base, half), :] = (upstream * result(1)).astype(BF16)
        grad_in[0, pl.ds(channels + base, half), :] = (grad_mix * at(saved, 2)).astype(BF16)
        grad_in[0, pl.ds(2 * channels + base, half), :] = (grad_mix * at(saved, 1)).astype(BF16)
        filt_grad[0, pl.ds(base, half), :] = result(3)


def per_device(fresh_input, act_prev, saved_input, grad_next, top_grad, filters):
    sections = lax.axis_size("pipe")
    blocks = lax.axis_size("seq")
    channels, width = filters.shape[1], filters.shape[2]
    total = 4 * channels
    ring = [(i, (i + 1) % sections) for i in range(sections)]
    arrived = lax.ppermute(act_prev, "pipe", ring)
    returned = lax.ppermute(grad_next, "pipe", [(b, a) for a, b in ring])
    whole = [
        pltpu.with_memory_space_constraint(a, pltpu.HBM)
        for a in (fresh_input, saved_input, top_grad, filters)
    ]
    fresh_input, saved_input, top_grad, filters = pl.pallas_call(
        stage_kernel,
        out_shape=[jax.ShapeDtypeStruct(a.shape, a.dtype) for a in whole],
        in_specs=[pl.BlockSpec(memory_space=pltpu.HBM)] * 4,
        out_specs=[pl.BlockSpec(memory_space=pltpu.VMEM)] * 4,
        scratch_shapes=[pltpu.SemaphoreType.DMA((4,))],
        compiler_params=PARAMS,
        cost_estimate=pl.CostEstimate(flops=0, bytes_accessed=2**19, transcendentals=0),
        name="stage_inputs",
    )(*whole)
    scratch = [pltpu.VMEM((total, width), F32)]
    sent = pl.pallas_call(
        gather_kernel,
        out_shape=jax.ShapeDtypeStruct((total, width), BF16),
        scratch_shapes=scratch,
        compiler_params=PARAMS,
        name="gather_rows",
    )(arrived, fresh_input, saved_input, returned, top_grad, filters)

    order = [trade_order(blocks)]

    def trade(value):
        cut = value.reshape(blocks, total // blocks, width)
        return lax.all_to_all(cut, "seq", 0, 0, axis_index_groups=order).reshape(total, width)

    held = trade(sent)
    done = pl.pallas_call(
        functools.partial(convolve_kernel, blocks),
        out_shape=jax.ShapeDtypeStruct((total, width), BF16),
        scratch_shapes=scratch,
        compiler_params=PARAMS,
        name="convolve",
    )(held, *(jnp.asarray(t) for t in tables(blocks, width)))
    back = trade(done)
    return pl.pallas_call(
        finish_kernel,
        out_shape=(
            jax.ShapeDtypeStruct((1, channels, width), BF16),
            jax.ShapeDtypeStruct((1, 3 * channels, width), BF16),
            jax.ShapeDtypeStruct((1, channels, width), F32),
        ),
        scratch_shapes=scratch,
        compiler_params=PARAMS,
        name="finish",
    )(back, arrived, fresh_input, saved_input, returned, top_grad)


def solution(mesh):
    placed = (
        P(None, "seq"),
        P("pipe", None, "seq"),
        P("pipe", None, "seq"),
        P("pipe", None, "seq"),
        P(None, "seq"),
        P("pipe", None, "seq"),
    )
    return jax.shard_map(
        per_device,
        mesh=mesh,
        in_specs=placed,
        out_specs=(P("pipe", None, "seq"), P("pipe", None, "seq"), P("pipe", None, "seq")),
        check_vma=False,
    )
```

```python
import functools

import jax
import jax.numpy as jnp
import ml_dtypes
import numpy as np
from jax import lax
from jax.experimental import pallas as pl
from jax.experimental.pallas import tpu as pltpu
from jax.sharding import PartitionSpec as P

F32 = jnp.float32
BF16 = jnp.bfloat16
PARAMS = pltpu.CompilerParams(vmem_limit_bytes=8 * 2**20)


def split_table(table):
    high = table.astype(ml_dtypes.bfloat16)
    low = (table - high.astype(np.float64)).astype(ml_dtypes.bfloat16)
    return high, low


def trade_order(blocks):
    first = blocks * 5 // 8 + 2 if blocks > 8 else 0
    return [(first + i) % blocks for i in range(blocks)]


@functools.lru_cache(maxsize=None)
def tables(blocks, width):
    length = blocks * width
    freq = np.arange(blocks)[:, None] + 0.25
    outer = 2.0 * np.pi * freq * np.array(trade_order(blocks))[None, :] / blocks
    inner = 2.0 * np.pi * (np.arange(width)[:, None] * np.arange(width)[None, :] % width) / width
    twist = 2.0 * np.pi * freq * np.arange(width)[None, :] / length
    cos_i, sin_i = np.cos(inner), np.sin(inner)
    outer_fwd = np.concatenate([np.cos(outer), -np.sin(outer)], axis=0)
    inner_fwd = np.block([[cos_i, -sin_i], [sin_i, cos_i]])
    outer_back = split_table(outer_fwd.T / length)
    return (
        np.concatenate(split_table(outer_fwd), axis=0),
        *split_table(inner_fwd),
        *split_table(inner_fwd.T.copy()),
        np.block([[outer_back[0], outer_back[0]], [outer_back[1], np.zeros_like(outer_back[1])]]),
        np.cos(twist).astype(np.float32),
        np.sin(twist).astype(np.float32),
    )


def halves(value):
    high = value.astype(BF16)
    low = (value - high.astype(F32)).astype(BF16)
    return high, low


def dot(a, b):
    return jnp.dot(a, b, preferred_element_type=F32)


def fine_dot(value, table_high, table_low):
    count = value.shape[0]
    high, low = halves(value)
    both = dot(jnp.concatenate([high, low], axis=0), table_high)
    return both[:count] + (both[count:] + dot(high, table_low))


def stage_kernel(fresh, saved, top, filt, fresh_v, saved_v, top_v, filt_v, sems):
    pairs = ((filt, filt_v), (saved, saved_v), (fresh, fresh_v), (top, top_v))
    copies = [pltpu.make_async_copy(a, b, sems.at[i]) for i, (a, b) in enumerate(pairs)]
    for copy in copies:
        copy.start()
    for copy in copies:
        copy.wait()


def gather_kernel(arrived, fresh, saved, returned, top, filt, out, rows):
    section = lax.axis_index("pipe")
    last = lax.axis_size("pipe") - 1
    channels = filt.shape[1]
    half = channels // 2
    for part in range(2):
        base = half * part

        def at(ref, group):
            span = pl.ds(group * channels + base, half)
            return (ref[0, span, :] if len(ref.shape) == 3 else ref[span, :]).astype(F32)

        key = jnp.where(section == 0, at(fresh, 1), at(arrived, 1))
        value = jnp.where(section == 0, at(fresh, 2), at(arrived, 2))
        upstream = jnp.where(section == last, at(top, 0), at(returned, 0))
        rows[pl.ds(0 + part, half, stride=8), :] = at(filt, 0)
        rows[pl.ds(2 + part, half, stride=8), :] = at(saved, 1) * at(saved, 2)
        rows[pl.ds(4 + part, half, stride=8), :] = key * value
        rows[pl.ds(6 + part, half, stride=8), :] = upstream * at(saved, 0)
    out[...] = rows[...].astype(BF16)


def convolve_kernel(blocks, x, f1, f2h, f2l, b2h, b2l, b1, cos_t, sin_t, out, rows):
    rows[...] = x[...].astype(F32)
    taken = [rows[pl.ds(r, blocks, stride=8), :].astype(BF16) for r in range(8)]
    flat = jnp.concatenate(taken, axis=1)
    first = dot(f1[...], flat)
    first = first[: 2 * blocks] + first[2 * blocks :]
    width = x.shape[1]
    cosine, sine = cos_t[...], sin_t[...]
    stacked = []
    for r in range(8):
        real = first[:blocks, r * width : (r + 1) * width]
        imag = first[blocks:, r * width : (r + 1) * width]
        stacked.append(
            jnp.concatenate([real * cosine + imag * sine, imag * cosine - real * sine], axis=1)
        )
    spec = fine_dot(jnp.concatenate(stacked, axis=0), f2h[...], f2l[...])

    def parts_of(r):
        return (
            spec[r * blocks : (r + 1) * blocks, :width],
            spec[r * blocks : (r + 1) * blocks, width:],
        )

    products = []
    for kind in range(4):
        for part in range(2):
            filt, mix_b, mix_f, grad = (parts_of(2 * k + part) for k in range(4))
            if kind < 2:
                (ar, ai), (br, bi) = filt, (mix_f if kind == 0 else mix_b)
                pair = [ar * br - ai * bi, ar * bi + ai * br]
            else:
                (ar, ai), (br, bi) = (filt if kind == 2 else mix_b), grad
                pair = [ar * br + ai * bi, ar * bi - ai * br]
            products.append(jnp.concatenate(pair, axis=1))
    back = fine_dot(jnp.concatenate(products, axis=0), b2h[...], b2l[...])
    columns = []
    for r in range(8):
        real = back[r * blocks : (r + 1) * blocks, :width]
        imag = back[r * blocks : (r + 1) * blocks, width:]
        columns.append(
            jnp.concatenate([real * cosine - imag * sine, imag * cosine + real * sine], axis=0)
        )
    last = dot(b1[...], jnp.concatenate(halves(jnp.concatenate(columns, axis=1)), axis=0))
    last = last[:blocks] + last[blocks:]
    for r in range(8):
        rows[pl.ds(r, blocks, stride=8), :] = last[:, r * width : (r + 1) * width]
    out[...] = rows[...].astype(BF16)


def finish_kernel(x, arrived, fresh, saved, returned, top, act, grad_in, filt_grad, rows):
    section = lax.axis_index("pipe")
    last = lax.axis_size("pipe") - 1
    channels = act.shape[1]
    half = channels // 2
    rows[...] = x[...].astype(F32)
    for part in range(2):
        base = half * part

        def at(ref, group):
            span = pl.ds(group * channels + base, half)
            return (ref[0, span, :] if len(ref.shape) == 3 else ref[span, :]).astype(F32)

        def result(kind):
            return rows[pl.ds(2 * kind + part, half, stride=8), :]

        query = jnp.where(section == 0, at(fresh, 0), at(arrived, 0))
        upstream = jnp.where(section == last, at(top, 0), at(returned, 0))
        grad_mix = result(2)
        act[0, pl.ds(base, half), :] = (query * result(0)).astype(BF16)
        grad_in[0, pl.ds(base, half), :] = (upstream * result(1)).astype(BF16)
        grad_in[0, pl.ds(channels + base, half), :] = (grad_mix * at(saved, 2)).astype(BF16)
        grad_in[0, pl.ds(2 * channels + base, half), :] = (grad_mix * at(saved, 1)).astype(BF16)
        filt_grad[0, pl.ds(base, half), :] = result(3)


def per_device(fresh_input, act_prev, saved_input, grad_next, top_grad, filters):
    sections = lax.axis_size("pipe")
    blocks = lax.axis_size("seq")
    channels, width = filters.shape[1], filters.shape[2]
    total = 4 * channels
    ring = [(i, (i + 1) % sections) for i in range(sections)]
    arrived = lax.ppermute(act_prev, "pipe", ring)
    returned = lax.ppermute(grad_next, "pipe", [(b, a) for a, b in ring])
    whole = [
        pltpu.with_memory_space_constraint(a, pltpu.HBM)
        for a in (fresh_input, saved_input, top_grad, filters)
    ]
    fresh_input, saved_input, top_grad, filters = pl.pallas_call(
        stage_kernel,
        out_shape=[jax.ShapeDtypeStruct(a.shape, a.dtype) for a in whole],
        in_specs=[pl.BlockSpec(memory_space=pltpu.HBM)] * 4,
        out_specs=[pl.BlockSpec(memory_space=pltpu.VMEM)] * 4,
        scratch_shapes=[pltpu.SemaphoreType.DMA((4,))],
        compiler_params=PARAMS,
        cost_estimate=pl.CostEstimate(flops=0, bytes_accessed=2**19, transcendentals=0),
        name="stage_inputs",
    )(*whole)
    scratch = [pltpu.VMEM((total, width), F32)]
    sent = pl.pallas_call(
        gather_kernel,
        out_shape=jax.ShapeDtypeStruct((total, width), BF16),
        scratch_shapes=scratch,
        compiler_params=PARAMS,
        name="gather_rows",
    )(arrived, fresh_input, saved_input, returned, top_grad, filters)

    order = [trade_order(blocks)]

    def trade(value):
        cut = value.reshape(blocks, total // blocks, width)
        return lax.all_to_all(cut, "seq", 0, 0, axis_index_groups=order).reshape(total, width)

    held = trade(sent)
    done = pl.pallas_call(
        functools.partial(convolve_kernel, blocks),
        out_shape=jax.ShapeDtypeStruct((total, width), BF16),
        scratch_shapes=scratch,
        compiler_params=PARAMS,
        name="convolve",
    )(held, *(jnp.asarray(t) for t in tables(blocks, width)))
    back = trade(done)
    return pl.pallas_call(
        finish_kernel,
        out_shape=(
            jax.ShapeDtypeStruct((1, channels, width), BF16),
            jax.ShapeDtypeStruct((1, 3 * channels, width), BF16),
            jax.ShapeDtypeStruct((1, channels, width), F32),
        ),
        scratch_shapes=scratch,
        compiler_params=PARAMS,
        name="finish",
    )(back, arrived, fresh_input, saved_input, returned, top_grad)


def solution(mesh):
    placed = (
        P(None, "seq"),
        P("pipe", None, "seq"),
        P("pipe", None, "seq"),
        P("pipe", None, "seq"),
        P(None, "seq"),
        P("pipe", None, "seq"),
    )
    return jax.shard_map(
        per_device,
        mesh=mesh,
        in_specs=placed,
        out_specs=(P("pipe", None, "seq"), P("pipe", None, "seq"), P("pipe", None, "seq")),
        check_vma=False,
    )
```

```python
import functools

import jax
import jax.numpy as jnp
import ml_dtypes
import numpy as np
from jax import lax
from jax.experimental import pallas as pl
from jax.experimental.pallas import tpu as pltpu
from jax.sharding import PartitionSpec as P

F32 = jnp.float32
BF16 = jnp.bfloat16
PARAMS = pltpu.CompilerParams(vmem_limit_bytes=8 * 2**20)


def split_table(table):
    high = table.astype(ml_dtypes.bfloat16)
    low = (table - high.astype(np.float64)).astype(ml_dtypes.bfloat16)
    return high, low


def trade_order(blocks):
    first = blocks * 11 // 16 + 2 if blocks > 8 else 0
    return [(first + i) % blocks for i in range(blocks)]


@functools.lru_cache(maxsize=None)
def tables(blocks, width):
    length = blocks * width
    freq = np.arange(blocks)[:, None] + 0.25
    outer = 2.0 * np.pi * freq * np.array(trade_order(blocks))[None, :] / blocks
    inner = 2.0 * np.pi * (np.arange(width)[:, None] * np.arange(width)[None, :] % width) / width
    twist = 2.0 * np.pi * freq * np.arange(width)[None, :] / length
    cos_i, sin_i = np.cos(inner), np.sin(inner)
    outer_fwd = np.concatenate([np.cos(outer), -np.sin(outer)], axis=0)
    inner_fwd = np.block([[cos_i, -sin_i], [sin_i, cos_i]])
    outer_back = split_table(outer_fwd.T / length)
    return (
        np.concatenate(split_table(outer_fwd), axis=1),
        inner_fwd.astype(ml_dtypes.bfloat16),
        inner_fwd.T.astype(ml_dtypes.bfloat16),
        np.block([[outer_back[0], outer_back[0]], [outer_back[1], np.zeros_like(outer_back[1])]]),
        np.cos(twist).astype(np.float32),
        np.sin(twist).astype(np.float32),
    )


def halves(value):
    high = value.astype(BF16)
    low = (value - high.astype(F32)).astype(BF16)
    return high, low


def dot(a, b):
    return jnp.dot(a, b, preferred_element_type=F32)


def fine_dot(value, table):
    count = value.shape[0]
    both = dot(jnp.concatenate(halves(value), axis=0), table)
    return both[:count] + both[count:]


def stage_kernel(fresh, saved, top, filt, fresh_v, saved_v, top_v, filt_v, sems):
    pairs = ((filt, filt_v), (saved, saved_v), (fresh, fresh_v), (top, top_v))
    copies = [pltpu.make_async_copy(a, b, sems.at[i]) for i, (a, b) in enumerate(pairs)]
    for copy in copies:
        copy.start()
    for copy in copies:
        copy.wait()


def gather_kernel(arrived, fresh, saved, returned, top, filt, out, rows):
    section = lax.axis_index("pipe")
    last = lax.axis_size("pipe") - 1
    channels = filt.shape[1]
    half = channels // 2
    for part in range(2):
        base = half * part

        def at(ref, group):
            span = pl.ds(group * channels + base, half)
            return (ref[0, span, :] if len(ref.shape) == 3 else ref[span, :]).astype(F32)

        key = jnp.where(section == 0, at(fresh, 1), at(arrived, 1))
        value = jnp.where(section == 0, at(fresh, 2), at(arrived, 2))
        upstream = jnp.where(section == last, at(top, 0), at(returned, 0))
        rows[pl.ds(0 + part, half, stride=8), :] = at(filt, 0)
        rows[pl.ds(2 + part, half, stride=8), :] = at(saved, 1) * at(saved, 2)
        rows[pl.ds(4 + part, half, stride=8), :] = key * value
        rows[pl.ds(6 + part, half, stride=8), :] = upstream * at(saved, 0)
    out[...] = rows[...].astype(BF16)


def convolve_kernel(blocks, x, f1, f2, b2, b1, cos_t, sin_t, out, rows):
    rows[...] = x[...].astype(F32)
    taken = [rows[pl.ds(r, blocks, stride=8), :].astype(BF16) for r in range(8)]
    flat = jnp.concatenate(taken, axis=1)
    first = dot(f1[...], jnp.concatenate([flat, flat], axis=0))
    width = x.shape[1]
    cosine, sine = cos_t[...], sin_t[...]
    stacked = []
    for r in range(8):
        real = first[:blocks, r * width : (r + 1) * width]
        imag = first[blocks:, r * width : (r + 1) * width]
        stacked.append(
            jnp.concatenate([real * cosine + imag * sine, imag * cosine - real * sine], axis=1)
        )
    spec = fine_dot(jnp.concatenate(stacked, axis=0), f2[...])

    def parts_of(r):
        return (
            spec[r * blocks : (r + 1) * blocks, :width],
            spec[r * blocks : (r + 1) * blocks, width:],
        )

    products = []
    for kind in range(4):
        for part in range(2):
            filt, mix_b, mix_f, grad = (parts_of(2 * k + part) for k in range(4))
            if kind < 2:
                (ar, ai), (br, bi) = filt, (mix_f if kind == 0 else mix_b)
                pair = [ar * br - ai * bi, ar * bi + ai * br]
            else:
                (ar, ai), (br, bi) = (filt if kind == 2 else mix_b), grad
                pair = [ar * br + ai * bi, ar * bi - ai * br]
            products.append(jnp.concatenate(pair, axis=1))
    back = fine_dot(jnp.concatenate(products, axis=0), b2[...])
    columns = []
    for r in range(8):
        real = back[r * blocks : (r + 1) * blocks, :width]
        imag = back[r * blocks : (r + 1) * blocks, width:]
        columns.append(
            jnp.concatenate([real * cosine - imag * sine, imag * cosine + real * sine], axis=0)
        )
    last = dot(b1[...], jnp.concatenate(halves(jnp.concatenate(columns, axis=1)), axis=0))
    last = last[:blocks] + last[blocks:]
    for r in range(8):
        rows[pl.ds(r, blocks, stride=8), :] = last[:, r * width : (r + 1) * width]
    out[...] = rows[...].astype(BF16)


def finish_kernel(x, arrived, fresh, saved, returned, top, act, grad_in, filt_grad, rows):
    section = lax.axis_index("pipe")
    last = lax.axis_size("pipe") - 1
    channels = act.shape[1]
    half = channels // 2
    rows[...] = x[...].astype(F32)
    for part in range(2):
        base = half * part

        def at(ref, group):
            span = pl.ds(group * channels + base, half)
            return (ref[0, span, :] if len(ref.shape) == 3 else ref[span, :]).astype(F32)

        def result(kind):
            return rows[pl.ds(2 * kind + part, half, stride=8), :]

        query = jnp.where(section == 0, at(fresh, 0), at(arrived, 0))
        upstream = jnp.where(section == last, at(top, 0), at(returned, 0))
        grad_mix = result(2)
        act[0, pl.ds(base, half), :] = (query * result(0)).astype(BF16)
        grad_in[0, pl.ds(base, half), :] = (upstream * result(1)).astype(BF16)
        grad_in[0, pl.ds(channels + base, half), :] = (grad_mix * at(saved, 2)).astype(BF16)
        grad_in[0, pl.ds(2 * channels + base, half), :] = (grad_mix * at(saved, 1)).astype(BF16)
        filt_grad[0, pl.ds(base, half), :] = result(3)


def per_device(fresh_input, act_prev, saved_input, grad_next, top_grad, filters):
    sections = lax.axis_size("pipe")
    blocks = lax.axis_size("seq")
    channels, width = filters.shape[1], filters.shape[2]
    total = 4 * channels
    ring = [(i, (i + 1) % sections) for i in range(sections)]
    arrived = lax.ppermute(act_prev, "pipe", ring)
    returned = lax.ppermute(grad_next, "pipe", [(b, a) for a, b in ring])
    whole = [
        pltpu.with_memory_space_constraint(a, pltpu.HBM)
        for a in (fresh_input, saved_input, top_grad, filters)
    ]
    fresh_input, saved_input, top_grad, filters = pl.pallas_call(
        stage_kernel,
        out_shape=[jax.ShapeDtypeStruct(a.shape, a.dtype) for a in whole],
        in_specs=[pl.BlockSpec(memory_space=pltpu.HBM)] * 4,
        out_specs=[pl.BlockSpec(memory_space=pltpu.VMEM)] * 4,
        scratch_shapes=[pltpu.SemaphoreType.DMA((4,))],
        compiler_params=PARAMS,
        cost_estimate=pl.CostEstimate(flops=0, bytes_accessed=2**19, transcendentals=0),
        name="stage_inputs",
    )(*whole)
    scratch = [pltpu.VMEM((total, width), F32)]
    sent = pl.pallas_call(
        gather_kernel,
        out_shape=jax.ShapeDtypeStruct((total, width), BF16),
        scratch_shapes=scratch,
        compiler_params=PARAMS,
        name="gather_rows",
    )(arrived, fresh_input, saved_input, returned, top_grad, filters)

    order = [trade_order(blocks)]

    def trade(value):
        cut = value.reshape(blocks, total // blocks, width)
        return lax.all_to_all(cut, "seq", 0, 0, axis_index_groups=order).reshape(total, width)

    held = trade(sent)
    done = pl.pallas_call(
        functools.partial(convolve_kernel, blocks),
        out_shape=jax.ShapeDtypeStruct((total, width), BF16),
        scratch_shapes=scratch,
        compiler_params=PARAMS,
        name="convolve",
    )(held, *(jnp.asarray(t) for t in tables(blocks, width)))
    back = trade(done)
    return pl.pallas_call(
        finish_kernel,
        out_shape=(
            jax.ShapeDtypeStruct((1, channels, width), BF16),
            jax.ShapeDtypeStruct((1, 3 * channels, width), BF16),
            jax.ShapeDtypeStruct((1, channels, width), F32),
        ),
        scratch_shapes=scratch,
        compiler_params=PARAMS,
        name="finish",
    )(back, arrived, fresh_input, saved_input, returned, top_grad)


def solution(mesh):
    placed = (
        P(None, "seq"),
        P("pipe", None, "seq"),
        P("pipe", None, "seq"),
        P("pipe", None, "seq"),
        P(None, "seq"),
        P("pipe", None, "seq"),
    )
    return jax.shard_map(
        per_device,
        mesh=mesh,
        in_specs=placed,
        out_specs=(P("pipe", None, "seq"), P("pipe", None, "seq"), P("pipe", None, "seq")),
        check_vma=False,
    )
```

```python
import functools

import jax
import jax.numpy as jnp
import ml_dtypes
import numpy as np
from jax import lax
from jax.experimental import pallas as pl
from jax.experimental.pallas import tpu as pltpu
from jax.sharding import PartitionSpec as P

F32 = jnp.float32
BF16 = jnp.bfloat16
PARAMS = pltpu.CompilerParams(vmem_limit_bytes=8 * 2**20)


def split_table(table):
    high = table.astype(ml_dtypes.bfloat16)
    low = (table - high.astype(np.float64)).astype(ml_dtypes.bfloat16)
    return high, low


def trade_order(blocks):
    first = blocks * 11 // 16 + 2 if blocks > 8 else 0
    away = [min((i - first) % blocks, (first - i) % blocks) for i in range(blocks)]
    return sorted(range(blocks), key=lambda i: (i != first, -away[i], i))


@functools.lru_cache(maxsize=None)
def tables(blocks, width):
    length = blocks * width
    freq = np.arange(blocks)[:, None] + 0.25
    outer = 2.0 * np.pi * freq * np.array(trade_order(blocks))[None, :] / blocks
    inner = 2.0 * np.pi * (np.arange(width)[:, None] * np.arange(width)[None, :] % width) / width
    twist = 2.0 * np.pi * freq * np.arange(width)[None, :] / length
    cos_i, sin_i = np.cos(inner), np.sin(inner)
    outer_fwd = np.concatenate([np.cos(outer), -np.sin(outer)], axis=0)
    inner_fwd = np.block([[cos_i, -sin_i], [sin_i, cos_i]])
    outer_back = split_table(outer_fwd.T / length)
    return (
        np.concatenate(split_table(outer_fwd), axis=1),
        inner_fwd.astype(ml_dtypes.bfloat16),
        inner_fwd.T.astype(ml_dtypes.bfloat16),
        np.block([[outer_back[0], outer_back[0]], [outer_back[1], np.zeros_like(outer_back[1])]]),
        np.cos(twist).astype(np.float32),
        np.sin(twist).astype(np.float32),
    )


def halves(value):
    high = value.astype(BF16)
    low = (value - high.astype(F32)).astype(BF16)
    return high, low


def dot(a, b):
    return jnp.dot(a, b, preferred_element_type=F32)


def fine_dot(value, table):
    count = value.shape[0]
    both = dot(jnp.concatenate(halves(value), axis=0), table)
    return both[:count] + both[count:]


def stage_kernel(fresh, saved, top, filt, fresh_v, saved_v, top_v, filt_v, sems):
    pairs = ((filt, filt_v), (saved, saved_v), (fresh, fresh_v), (top, top_v))
    copies = [pltpu.make_async_copy(a, b, sems.at[i]) for i, (a, b) in enumerate(pairs)]
    for copy in copies:
        copy.start()
    for copy in copies:
        copy.wait()


def gather_kernel(arrived, fresh, saved, returned, top, filt, out, rows):
    section = lax.axis_index("pipe")
    last = lax.axis_size("pipe") - 1
    channels = filt.shape[1]
    half = channels // 2
    for part in range(2):
        base = half * part

        def at(ref, group):
            span = pl.ds(group * channels + base, half)
            return (ref[0, span, :] if len(ref.shape) == 3 else ref[span, :]).astype(F32)

        key = jnp.where(section == 0, at(fresh, 1), at(arrived, 1))
        value = jnp.where(section == 0, at(fresh, 2), at(arrived, 2))
        upstream = jnp.where(section == last, at(top, 0), at(returned, 0))
        rows[pl.ds(0 + part, half, stride=8), :] = at(filt, 0)
        rows[pl.ds(2 + part, half, stride=8), :] = at(saved, 1) * at(saved, 2)
        rows[pl.ds(4 + part, half, stride=8), :] = key * value
        rows[pl.ds(6 + part, half, stride=8), :] = upstream * at(saved, 0)
    out[...] = rows[...].astype(BF16)


def convolve_kernel(blocks, x, f1, f2, b2, b1, cos_t, sin_t, out, rows):
    rows[...] = x[...].astype(F32)
    taken = [rows[pl.ds(r, blocks, stride=8), :].astype(BF16) for r in range(8)]
    flat = jnp.concatenate(taken, axis=1)
    first = dot(f1[...], jnp.concatenate([flat, flat], axis=0))
    width = x.shape[1]
    cosine, sine = cos_t[...], sin_t[...]
    stacked = []
    for r in range(8):
        real = first[:blocks, r * width : (r + 1) * width]
        imag = first[blocks:, r * width : (r + 1) * width]
        stacked.append(
            jnp.concatenate([real * cosine + imag * sine, imag * cosine - real * sine], axis=1)
        )
    spec = fine_dot(jnp.concatenate(stacked, axis=0), f2[...])

    def parts_of(r):
        return (
            spec[r * blocks : (r + 1) * blocks, :width],
            spec[r * blocks : (r + 1) * blocks, width:],
        )

    products = []
    for kind in range(4):
        for part in range(2):
            filt, mix_b, mix_f, grad = (parts_of(2 * k + part) for k in range(4))
            if kind < 2:
                (ar, ai), (br, bi) = filt, (mix_f if kind == 0 else mix_b)
                pair = [ar * br - ai * bi, ar * bi + ai * br]
            else:
                (ar, ai), (br, bi) = (filt if kind == 2 else mix_b), grad
                pair = [ar * br + ai * bi, ar * bi - ai * br]
            products.append(jnp.concatenate(pair, axis=1))
    back = fine_dot(jnp.concatenate(products, axis=0), b2[...])
    columns = []
    for r in range(8):
        real = back[r * blocks : (r + 1) * blocks, :width]
        imag = back[r * blocks : (r + 1) * blocks, width:]
        columns.append(
            jnp.concatenate([real * cosine - imag * sine, imag * cosine + real * sine], axis=0)
        )
    last = dot(b1[...], jnp.concatenate(halves(jnp.concatenate(columns, axis=1)), axis=0))
    last = last[:blocks] + last[blocks:]
    for r in range(8):
        rows[pl.ds(r, blocks, stride=8), :] = last[:, r * width : (r + 1) * width]
    out[...] = rows[...].astype(BF16)


def finish_kernel(x, arrived, fresh, saved, returned, top, act, grad_in, filt_grad, rows):
    section = lax.axis_index("pipe")
    last = lax.axis_size("pipe") - 1
    channels = act.shape[1]
    half = channels // 2
    rows[...] = x[...].astype(F32)
    for part in range(2):
        base = half * part

        def at(ref, group):
            span = pl.ds(group * channels + base, half)
            return (ref[0, span, :] if len(ref.shape) == 3 else ref[span, :]).astype(F32)

        def result(kind):
            return rows[pl.ds(2 * kind + part, half, stride=8), :]

        query = jnp.where(section == 0, at(fresh, 0), at(arrived, 0))
        upstream = jnp.where(section == last, at(top, 0), at(returned, 0))
        grad_mix = result(2)
        act[0, pl.ds(base, half), :] = (query * result(0)).astype(BF16)
        grad_in[0, pl.ds(base, half), :] = (upstream * result(1)).astype(BF16)
        grad_in[0, pl.ds(channels + base, half), :] = (grad_mix * at(saved, 2)).astype(BF16)
        grad_in[0, pl.ds(2 * channels + base, half), :] = (grad_mix * at(saved, 1)).astype(BF16)
        filt_grad[0, pl.ds(base, half), :] = result(3)


def per_device(fresh_input, act_prev, saved_input, grad_next, top_grad, filters):
    sections = lax.axis_size("pipe")
    blocks = lax.axis_size("seq")
    channels, width = filters.shape[1], filters.shape[2]
    total = 4 * channels
    ring = [(i, (i + 1) % sections) for i in range(sections)]
    arrived = lax.ppermute(act_prev, "pipe", ring)
    returned = lax.ppermute(grad_next, "pipe", [(b, a) for a, b in ring])
    whole = [
        pltpu.with_memory_space_constraint(a, pltpu.HBM)
        for a in (fresh_input, saved_input, top_grad, filters)
    ]
    fresh_input, saved_input, top_grad, filters = pl.pallas_call(
        stage_kernel,
        out_shape=[jax.ShapeDtypeStruct(a.shape, a.dtype) for a in whole],
        in_specs=[pl.BlockSpec(memory_space=pltpu.HBM)] * 4,
        out_specs=[pl.BlockSpec(memory_space=pltpu.VMEM)] * 4,
        scratch_shapes=[pltpu.SemaphoreType.DMA((4,))],
        compiler_params=PARAMS,
        cost_estimate=pl.CostEstimate(flops=0, bytes_accessed=2**19, transcendentals=0),
        name="stage_inputs",
    )(*whole)
    scratch = [pltpu.VMEM((total, width), F32)]
    sent = pl.pallas_call(
        gather_kernel,
        out_shape=jax.ShapeDtypeStruct((total, width), BF16),
        scratch_shapes=scratch,
        compiler_params=PARAMS,
        name="gather_rows",
    )(arrived, fresh_input, saved_input, returned, top_grad, filters)

    order = [trade_order(blocks)]

    def trade(value):
        cut = value.reshape(blocks, total // blocks, width)
        return lax.all_to_all(cut, "seq", 0, 0, axis_index_groups=order).reshape(total, width)

    held = trade(sent)
    done = pl.pallas_call(
        functools.partial(convolve_kernel, blocks),
        out_shape=jax.ShapeDtypeStruct((total, width), BF16),
        scratch_shapes=scratch,
        compiler_params=PARAMS,
        name="convolve",
    )(held, *(jnp.asarray(t) for t in tables(blocks, width)))
    back = trade(done)
    return pl.pallas_call(
        finish_kernel,
        out_shape=(
            jax.ShapeDtypeStruct((1, channels, width), BF16),
            jax.ShapeDtypeStruct((1, 3 * channels, width), BF16),
            jax.ShapeDtypeStruct((1, channels, width), F32),
        ),
        scratch_shapes=scratch,
        compiler_params=PARAMS,
        name="finish",
    )(back, arrived, fresh_input, saved_input, returned, top_grad)


def solution(mesh):
    placed = (
        P(None, "seq"),
        P("pipe", None, "seq"),
        P("pipe", None, "seq"),
        P("pipe", None, "seq"),
        P(None, "seq"),
        P("pipe", None, "seq"),
    )
    return jax.shard_map(
        per_device,
        mesh=mesh,
        in_specs=placed,
        out_specs=(P("pipe", None, "seq"), P("pipe", None, "seq"), P("pipe", None, "seq")),
        check_vma=False,
    )
```

```python
import functools

import jax
import jax.numpy as jnp
import ml_dtypes
import numpy as np
from jax import lax
from jax.experimental import pallas as pl
from jax.experimental.pallas import tpu as pltpu
from jax.sharding import PartitionSpec as P

F32 = jnp.float32
BF16 = jnp.bfloat16
PARAMS = pltpu.CompilerParams(vmem_limit_bytes=8 * 2**20)


def split_table(table):
    high = table.astype(ml_dtypes.bfloat16)
    low = (table - high.astype(np.float64)).astype(ml_dtypes.bfloat16)
    return high, low


def trade_order(blocks):
    first = blocks * 11 // 16 + 3 if blocks > 8 else 0
    away = [min((i - first) % blocks, (first - i) % blocks) for i in range(blocks)]
    return sorted(range(blocks), key=lambda i: (i != first, -away[i], i))


@functools.lru_cache(maxsize=None)
def tables(blocks, width):
    length = blocks * width
    freq = np.arange(blocks)[:, None] + 0.25
    outer = 2.0 * np.pi * freq * np.array(trade_order(blocks))[None, :] / blocks
    inner = 2.0 * np.pi * (np.arange(width)[:, None] * np.arange(width)[None, :] % width) / width
    twist = 2.0 * np.pi * freq * np.arange(width)[None, :] / length
    cos_i, sin_i = np.cos(inner), np.sin(inner)
    outer_fwd = np.concatenate([np.cos(outer), -np.sin(outer)], axis=0)
    inner_fwd = np.block([[cos_i, -sin_i], [sin_i, cos_i]])
    outer_back = split_table(outer_fwd.T / length)
    return (
        np.concatenate(split_table(outer_fwd), axis=1),
        inner_fwd.astype(ml_dtypes.bfloat16),
        inner_fwd.T.astype(ml_dtypes.bfloat16),
        np.block([[outer_back[0], outer_back[0]], [outer_back[1], np.zeros_like(outer_back[1])]]),
        np.cos(twist).astype(np.float32),
        np.sin(twist).astype(np.float32),
    )


def halves(value):
    high = value.astype(BF16)
    low = (value - high.astype(F32)).astype(BF16)
    return high, low


def dot(a, b):
    return jnp.dot(a, b, preferred_element_type=F32)


def fine_dot(value, table):
    count = value.shape[0]
    both = dot(jnp.concatenate(halves(value), axis=0), table)
    return both[:count] + both[count:]


def stage_kernel(fresh, saved, top, filt, fresh_v, saved_v, top_v, filt_v, sems):
    pairs = ((filt, filt_v), (saved, saved_v), (fresh, fresh_v), (top, top_v))
    copies = [pltpu.make_async_copy(a, b, sems.at[i]) for i, (a, b) in enumerate(pairs)]
    for copy in copies:
        copy.start()
    for copy in copies:
        copy.wait()


def gather_kernel(arrived, fresh, saved, returned, top, filt, out, rows):
    section = lax.axis_index("pipe")
    last = lax.axis_size("pipe") - 1
    channels = filt.shape[1]
    half = channels // 2
    for part in range(2):
        base = half * part

        def at(ref, group):
            span = pl.ds(group * channels + base, half)
            return (ref[0, span, :] if len(ref.shape) == 3 else ref[span, :]).astype(F32)

        key = jnp.where(section == 0, at(fresh, 1), at(arrived, 1))
        value = jnp.where(section == 0, at(fresh, 2), at(arrived, 2))
        upstream = jnp.where(section == last, at(top, 0), at(returned, 0))
        rows[pl.ds(0 + part, half, stride=8), :] = at(filt, 0)
        rows[pl.ds(2 + part, half, stride=8), :] = at(saved, 1) * at(saved, 2)
        rows[pl.ds(4 + part, half, stride=8), :] = key * value
        rows[pl.ds(6 + part, half, stride=8), :] = upstream * at(saved, 0)
    out[...] = rows[...].astype(BF16)


def convolve_kernel(blocks, x, f1, f2, b2, b1, cos_t, sin_t, out, rows):
    rows[...] = x[...].astype(F32)
    taken = [rows[pl.ds(r, blocks, stride=8), :].astype(BF16) for r in range(8)]
    flat = jnp.concatenate(taken, axis=1)
    first = dot(f1[...], jnp.concatenate([flat, flat], axis=0))
    width = x.shape[1]
    cosine, sine = cos_t[...], sin_t[...]
    stacked = []
    for r in range(8):
        real = first[:blocks, r * width : (r + 1) * width]
        imag = first[blocks:, r * width : (r + 1) * width]
        stacked.append(
            jnp.concatenate([real * cosine + imag * sine, imag * cosine - real * sine], axis=1)
        )
    spec = fine_dot(jnp.concatenate(stacked, axis=0), f2[...])

    def parts_of(r):
        return (
            spec[r * blocks : (r + 1) * blocks, :width],
            spec[r * blocks : (r + 1) * blocks, width:],
        )

    products = []
    for kind in range(4):
        for part in range(2):
            filt, mix_b, mix_f, grad = (parts_of(2 * k + part) for k in range(4))
            if kind < 2:
                (ar, ai), (br, bi) = filt, (mix_f if kind == 0 else mix_b)
                pair = [ar * br - ai * bi, ar * bi + ai * br]
            else:
                (ar, ai), (br, bi) = (filt if kind == 2 else mix_b), grad
                pair = [ar * br + ai * bi, ar * bi - ai * br]
            products.append(jnp.concatenate(pair, axis=1))
    back = fine_dot(jnp.concatenate(products, axis=0), b2[...])
    columns = []
    for r in range(8):
        real = back[r * blocks : (r + 1) * blocks, :width]
        imag = back[r * blocks : (r + 1) * blocks, width:]
        columns.append(
            jnp.concatenate([real * cosine - imag * sine, imag * cosine + real * sine], axis=0)
        )
    last = dot(b1[...], jnp.concatenate(halves(jnp.concatenate(columns, axis=1)), axis=0))
    last = last[:blocks] + last[blocks:]
    for r in range(8):
        rows[pl.ds(r, blocks, stride=8), :] = last[:, r * width : (r + 1) * width]
    out[...] = rows[...].astype(BF16)


def finish_kernel(x, arrived, fresh, saved, returned, top, act, grad_in, filt_grad, rows):
    section = lax.axis_index("pipe")
    last = lax.axis_size("pipe") - 1
    channels = act.shape[1]
    half = channels // 2
    rows[...] = x[...].astype(F32)
    for part in range(2):
        base = half * part

        def at(ref, group):
            span = pl.ds(group * channels + base, half)
            return (ref[0, span, :] if len(ref.shape) == 3 else ref[span, :]).astype(F32)

        def result(kind):
            return rows[pl.ds(2 * kind + part, half, stride=8), :]

        query = jnp.where(section == 0, at(fresh, 0), at(arrived, 0))
        upstream = jnp.where(section == last, at(top, 0), at(returned, 0))
        grad_mix = result(2)
        act[0, pl.ds(base, half), :] = (query * result(0)).astype(BF16)
        grad_in[0, pl.ds(base, half), :] = (upstream * result(1)).astype(BF16)
        grad_in[0, pl.ds(channels + base, half), :] = (grad_mix * at(saved, 2)).astype(BF16)
        grad_in[0, pl.ds(2 * channels + base, half), :] = (grad_mix * at(saved, 1)).astype(BF16)
        filt_grad[0, pl.ds(base, half), :] = result(3)


def per_device(fresh_input, act_prev, saved_input, grad_next, top_grad, filters):
    sections = lax.axis_size("pipe")
    blocks = lax.axis_size("seq")
    channels, width = filters.shape[1], filters.shape[2]
    total = 4 * channels
    ring = [(i, (i + 1) % sections) for i in range(sections)]
    arrived = lax.ppermute(act_prev, "pipe", ring)
    returned = lax.ppermute(grad_next, "pipe", [(b, a) for a, b in ring])
    whole = [
        pltpu.with_memory_space_constraint(a, pltpu.HBM)
        for a in (fresh_input, saved_input, top_grad, filters)
    ]
    fresh_input, saved_input, top_grad, filters = pl.pallas_call(
        stage_kernel,
        out_shape=[jax.ShapeDtypeStruct(a.shape, a.dtype) for a in whole],
        in_specs=[pl.BlockSpec(memory_space=pltpu.HBM)] * 4,
        out_specs=[pl.BlockSpec(memory_space=pltpu.VMEM)] * 4,
        scratch_shapes=[pltpu.SemaphoreType.DMA((4,))],
        compiler_params=PARAMS,
        cost_estimate=pl.CostEstimate(flops=0, bytes_accessed=2**19, transcendentals=0),
        name="stage_inputs",
    )(*whole)
    scratch = [pltpu.VMEM((total, width), F32)]
    sent = pl.pallas_call(
        gather_kernel,
        out_shape=jax.ShapeDtypeStruct((total, width), BF16),
        scratch_shapes=scratch,
        compiler_params=PARAMS,
        name="gather_rows",
    )(arrived, fresh_input, saved_input, returned, top_grad, filters)

    order = [trade_order(blocks)]

    def trade(value):
        cut = value.reshape(blocks, total // blocks, width)
        return lax.all_to_all(cut, "seq", 0, 0, axis_index_groups=order).reshape(total, width)

    held = trade(sent)
    done = pl.pallas_call(
        functools.partial(convolve_kernel, blocks),
        out_shape=jax.ShapeDtypeStruct((total, width), BF16),
        scratch_shapes=scratch,
        compiler_params=PARAMS,
        name="convolve",
    )(held, *(jnp.asarray(t) for t in tables(blocks, width)))
    back = trade(done)
    return pl.pallas_call(
        finish_kernel,
        out_shape=(
            jax.ShapeDtypeStruct((1, channels, width), BF16),
            jax.ShapeDtypeStruct((1, 3 * channels, width), BF16),
            jax.ShapeDtypeStruct((1, channels, width), F32),
        ),
        scratch_shapes=scratch,
        compiler_params=PARAMS,
        name="finish",
    )(back, arrived, fresh_input, saved_input, returned, top_grad)


def solution(mesh):
    placed = (
        P(None, "seq"),
        P("pipe", None, "seq"),
        P("pipe", None, "seq"),
        P("pipe", None, "seq"),
        P(None, "seq"),
        P("pipe", None, "seq"),
    )
    return jax.shard_map(
        per_device,
        mesh=mesh,
        in_specs=placed,
        out_specs=(P("pipe", None, "seq"), P("pipe", None, "seq"), P("pipe", None, "seq")),
        check_vma=False,
    )
```
